32 devices in a mesh: dp: 2 (over x), blk: 4 (over y, core), cent: 4 (over z).
Axes of the slice: x: 2, y: 2, z: 4, core: 2. Of those that a mesh axis runs over, the one named last changes fastest.
Arguments:
- embeddings: float32 [16384, 1024], P(('dp', 'blk', 'cent'))
- cluster_ids: int32 [16384, 1], P(('dp', 'blk', 'cent')), may hold values from 0 to 7; in each aligned block of 512 rows (0 to 511, 512 to 1023, ...) at most 96 rows name the same one
- order_index: int32 [16384], P(('dp', 'blk', 'cent')), may hold values from 0 to 16383, each once
- shard_counts: int32 [32], P(('dp', 'blk', 'cent')), may hold values from 1 to 512, 14336 in all
Outputs:
- best_cos: float32 [16384], P(('dp', 'blk', 'cent'))
- centroid: float32 [8, 1024], P(('dp', 'cent'), 'blk')
The draws below stay inside these ranges and needn't reach their ends.
Inputs may be any that keep to these rules, and one draw needn't show every extreme that they name: `cluster_ids`: among the 512 rows of one shard no cluster id appears more than 96 times, and some id appears exactly 96 times. `order_index`: all values are distinct.
All inputs are finite; a program needn't handle non-finite values. No bound on the sum of `shard_counts` on one device may be relied on, other than what follows from the above.
Results may differ from the reference program's by a relative error of at most 0.0003.
Values may be sent and summed in bfloat16 or wider, within the bound.
A program may use at most 64 MiB of HBM per device.

```python
import math
import jax
import jax.numpy as jnp
import numpy as np
from jax import lax

D = 1024
ROWS_SH = 512
SHARDS = 32
TOTAL = 16384
CLUSTERS = 8
CAP = 96
N_DP = 2
N_BLK = 4
N_CENT = 4


def draw_embeddings(key, part):
    key_family = jax.random.fold_in(key, 11)
    key_table = jax.random.fold_in(key, 12)
    key_strength = jax.random.fold_in(key, 13)
    key_noise = jax.random.fold_in(key, 14)
    family = jax.random.randint(key_family, (TOTAL,), 0, 256)
    family_table = jax.random.normal(key_table, (256, D), jnp.float32)
    strength = jnp.exp(jax.random.uniform(key_strength, (TOTAL, 1), jnp.float32, jnp.log(0.3), jnp.log(3.0)))
    noise_part = jax.random.normal(key_noise, (TOTAL, D), jnp.float32)
    return (noise_part + strength * family_table[family]).astype(jnp.float32)


def length_profile(number_of, total, reach, slope):
    weights = [(1 << 20) // math.isqrt(rank ** slope) + 1 for rank in range(2, number_of + 1)]
    rest, given = total - reach - (number_of - 1), [1] * (number_of - 1)
    while rest > 0:
        free = [i for i in range(number_of - 1) if given[i] < reach]
        mass, left = sum([weights[i] for i in free]), rest
        for i in free:
            more = min(reach - given[i], max(1, left * weights[i] // mass), rest)
            given[i] = given[i] + more
            rest = rest - more
    return np.array([reach] + given)


def uneven_parts(key, number_of, total, most, lean):
    if number_of == 2:
        one = jax.random.randint(key, (), max(1, total - most), min(most, total - 1) + 1)
        return jnp.stack([one, total - one])
    tallies = jnp.asarray(length_profile(number_of, total, most, lean), jnp.int32)
    pairs = (number_of - 1) // 2
    source_of, taker = tallies[1:1 + 2 * pairs:2], tallies[2:2 + 2 * pairs:2]
    margin = jnp.minimum(source_of - 1, most - taker)
    passed = jax.random.randint(jax.random.fold_in(key, 1), (pairs,), 0, 1 << 20) % (margin + 1)
    tallies = tallies.at[1:1 + 2 * pairs:2].set(source_of - passed).at[2:2 + 2 * pairs:2].set(taker + passed)
    return tallies[jax.random.permutation(jax.random.fold_in(key, 2), number_of)]


def routed_block(own_key, own, number, rows, number_of, top, limit, skew):
    sequence = jax.random.permutation(own_key, number_of)
    heavy_load, usual = load_shares(number_of, rows * top, limit, skew, True), load_shares(number_of, rows * top, limit, skew, False)
    places = jnp.arange(number_of)

    def named(lengths, rotation):
        used = int((lengths > 0).sum())
        fixed = max(1, used // 4)
        shifted = fixed + (places - fixed + rotation * (used - fixed)) % max(1, number_of - fixed)
        return jnp.zeros((number_of,), jnp.int32).at[sequence[jnp.where(places < fixed, places, shifted)]].set(jnp.asarray(lengths, jnp.int32))

    lengths = jnp.where(number % 4 == 0, named(heavy_load, number // 4), named(usual, number - number // 4 - 1))
    mixed = jax.random.permutation(jax.random.fold_in(own, 3), number_of)
    giver, taker = mixed[0:number_of // 2 * 2:2], mixed[1:number_of // 2 * 2:2]
    margin = jnp.minimum(lengths[giver] - 1, limit - lengths[taker]) // 2
    margin = jnp.where((giver == sequence[0]) | (taker == sequence[0]) | (lengths[taker] == 0), 0, jnp.maximum(margin, 0))
    shifted = jax.random.randint(jax.random.fold_in(own, 4), (number_of // 2,), 0, 1 << 20) % (margin + 1)
    lengths = lengths.at[giver].add(-shifted).at[taker].add(shifted)
    members = jnp.searchsorted(jnp.cumsum(lengths), jnp.arange(rows * top), side="right").astype(jnp.int32)
    table = members.reshape(top, rows).T
    table = table[jax.random.permutation(jax.random.fold_in(own, 1), rows)]
    rotation = jax.random.randint(jax.random.fold_in(own, 2), (rows, 1), 0, top)
    return jnp.take_along_axis(table, (jnp.arange(top)[None, :] + rotation) % top, axis=1)


def load_shares(amount, total, most, slope, full):
    weights = [(1 << 20) // math.isqrt(grade ** slope) + 1 for grade in range(1, amount + 1)]
    largest = most if full else min(most, max(-(-total // amount), total * weights[0] // sum(weights)))
    least = 1 if total - largest >= amount - 1 else 0
    counts, spare = [largest] + [least] * (amount - 1), total - largest - least * (amount - 1)
    while spare > 0:
        movable = [i for i in range(1, amount) if counts[i] < largest] or [i for i in range(1, amount) if counts[i] < most]
        whole, budget = sum([weights[i] for i in movable]), spare
        for i in movable:
            addition = min(most - counts[i], max(1, budget * weights[i] // whole), spare)
            counts[i] = counts[i] + addition
            spare = spare - addition
    return np.array(counts)


def setup_inputs(seed: int = 0) -> dict:
    keys = jax.random.split(jax.random.key(seed), 5)
    embeddings = draw_embeddings(jax.random.fold_in(keys[4], 71), 0)
    cluster_ids_keys = jax.random.split(jax.random.fold_in(keys[1], 1), TOTAL // ROWS_SH)
    cluster_ids_turns = jax.random.permutation(jax.random.fold_in(keys[1], 3), TOTAL // ROWS_SH)
    cluster_ids = jax.vmap(lambda own, number: routed_block(jax.random.fold_in(keys[1], 2), own, number, ROWS_SH, CLUSTERS, 1, CAP, 1))(cluster_ids_keys, cluster_ids_turns).reshape((TOTAL, 1))
    order_index = jax.random.permutation(keys[2], TOTAL).astype(jnp.int32)
    shard_counts = uneven_parts(keys[3], SHARDS, SHARDS * ROWS_SH * 7 // 8, ROWS_SH, 1).astype(jnp.int32)
    return {"embeddings": embeddings, "cluster_ids": cluster_ids, "order_index": order_index, "shard_counts": shard_counts}


epsilon = 1e-06

def reference(embeddings, cluster_ids, order_index, shard_counts):
    total_rows = embeddings.shape[0]
    capacity = N_DP * N_BLK * N_CENT * CAP
    position = jnp.arange(total_rows, dtype=jnp.int32)
    limits = jnp.repeat(shard_counts, ROWS_SH, total_repeat_length=total_rows)
    member_flag = position % ROWS_SH < limits
    cluster_col = jnp.where(member_flag, cluster_ids[:, 0], CLUSTERS).astype(jnp.int32)
    inverse = lax.rsqrt(lax.optimization_barrier(jnp.mean(embeddings * embeddings, axis=1)) + epsilon) / jnp.sqrt(jnp.float32(D))
    normed = (embeddings * inverse[:, None]).astype(jnp.bfloat16)
    order_perm = jnp.argsort(cluster_col, stable=True).astype(jnp.int32)
    onehot = (cluster_col[:, None] == jnp.arange(CLUSTERS, dtype=jnp.int32)[None, :]).astype(jnp.int32)
    cluster_sizes = lax.optimization_barrier(jnp.sum(onehot, axis=0)).astype(jnp.int32)
    starts = (jnp.cumsum(cluster_sizes) - cluster_sizes).astype(jnp.int32)
    sorted_norm = jnp.concatenate([normed[order_perm], jnp.zeros((capacity, D), jnp.bfloat16)], axis=0)
    sorted_raw = jnp.concatenate([embeddings[order_perm], jnp.zeros((capacity, D), embeddings.dtype)], axis=0)
    sorted_order = jnp.concatenate([order_index[order_perm], jnp.zeros((capacity,), jnp.int32)], axis=0).astype(jnp.int32)
    sorted_cluster = jnp.concatenate([cluster_col[order_perm], jnp.full((capacity,), CLUSTERS, jnp.int32)], axis=0).astype(jnp.int32)

    def per_cluster(index):
        first = starts[index].astype(jnp.int32)
        rows_norm = lax.dynamic_slice_in_dim(sorted_norm, first, capacity, 0).astype(jnp.float32)
        rows_raw = lax.dynamic_slice_in_dim(sorted_raw, first, capacity, 0)
        order_slice = lax.dynamic_slice_in_dim(sorted_order, first, capacity, 0)
        cluster_slice = lax.dynamic_slice_in_dim(sorted_cluster, first, capacity, 0)
        live = cluster_slice == index
        scores = jnp.dot(rows_norm, rows_norm.T, precision=lax.Precision.HIGHEST)
        earlier = live[None, :] & (order_slice[None, :] < order_slice[:, None])
        running = lax.optimization_barrier(jnp.max(jnp.where(earlier, scores, -1.0), axis=1))
        running = jnp.maximum(running, -1.0)
        keep = jnp.where(live, jax.nn.sigmoid(10.0 * (0.5 - running)), 0.0)
        summed = jnp.dot(keep, rows_raw, precision=lax.Precision.HIGHEST)
        return (running, summed, jnp.sum(keep), live)
    maxima, sums, weights, lives = lax.map(per_cluster, jnp.arange(CLUSTERS, dtype=jnp.int32))
    targets = jnp.where(lives, starts[:, None] + jnp.arange(capacity, dtype=jnp.int32)[None, :], total_rows + capacity).astype(jnp.int32)
    sorted_best = jnp.zeros((total_rows,), maxima.dtype).at[targets.reshape(-1)].set(maxima.reshape(-1), mode='drop')
    best = jnp.zeros((total_rows,), maxima.dtype).at[order_perm].set(sorted_best)
    best_cos = jnp.where(member_flag, best, 0.0)
    centroid = sums / jnp.sqrt(1.0 + weights)[:, None]
    return (best_cos, centroid)
```

```python
import functools

import jax
import jax.numpy as jnp
from jax import lax
from jax.experimental import pallas as pl
from jax.experimental.pallas import tpu as pltpu
from jax.sharding import PartitionSpec as P

epsilon = 1e-06
sentinel = 1073741824.0
MESH = pl.DeviceIdType.MESH
NT = (((1,), (1,)), ((), ()))


def kernel(
    n_dp, n_blk, n_cent, capacity,
    emb, cid_ref, ord_ref, cnt_ref,
    best_ref, cent_ref,
    normed, emb_hi, emb_lo, pack, got, order_out, order_in, order_col,
    home_out, home_in, part, part_in, row_out, row_in,
    a_send, a_recv, o_send, o_recv, c_send, c_recv, y_send, y_recv, d_send, d_recv,
    p_send, p_recv, h_send, h_recv, r_send, r_recv, s_send, s_recv,
):
    groups = n_dp * n_cent
    rows, features = emb.shape
    slots = groups * capacity
    b = lax.axis_index("blk")
    g = lax.axis_index("dp") * n_cent + lax.axis_index("cent")
    chips = n_blk // 2
    other = b + 1 - 2 * lax.rem(b, 2)
    f32, bf16 = jnp.float32, jnp.bfloat16

    def group(index):
        return {"dp": index // n_cent, "cent": lax.rem(index, n_cent)}

    def peer(k):
        return lax.rem(g + k, groups)

    def source(k):
        return lax.rem(g + groups - k, groups)

    def block(index):
        return pl.ds(pl.multiple_of(index * capacity, capacity), capacity)

    def remote(src, dst, send, recv, device):
        return pltpu.make_async_remote_copy(
            src_ref=src, dst_ref=dst, send_sem=send, recv_sem=recv,
            device_id=device, device_id_type=MESH,
        )

    def rows_copy(k):
        return remote(pack.at[block(peer(k))], got.at[b, block(g)], a_send.at[k], a_recv.at[k], group(peer(k)))

    def order_copy(k):
        return remote(order_out.at[peer(k)], order_in.at[b, g], o_send.at[k], o_recv.at[k], group(peer(k)))

    def core_copy(k):
        part_of = got.at[b, block(source(k))]
        return remote(part_of, part_of, c_send.at[k], c_recv.at[k], {"blk": other})

    def chip_copy(m, k):
        part_of = got.at[b, block(source(k))]
        return remote(part_of, part_of, y_send.at[m, k], y_recv.at[m, k], {"blk": lax.rem(b + 2 * m, n_blk)})

    def diagonal_copy(m, k):
        part_of = got.at[lax.rem(b + n_blk - 2 * m, n_blk), block(source(k))]
        return remote(part_of, part_of, d_send.at[m, k], d_recv.at[m, k], {"blk": other})

    def orders_copy(j):
        return remote(order_in.at[b], order_in.at[b], p_send.at[j], p_recv.at[j], {"blk": lax.rem(b + j, n_blk)})

    def home_copy(k):
        return remote(home_out.at[peer(k)], home_in.at[g], h_send.at[k], h_recv.at[k], group(peer(k)))

    def part_copy(j):
        return remote(
            part.at[lax.rem(b + j, n_blk)], part_in.at[b], r_send.at[j], r_recv.at[j], {"blk": lax.rem(b + j, n_blk)}
        )

    def row_copy(k):
        return remote(row_out.at[peer(k)], row_in.at[g], s_send.at[k], s_recv.at[k], group(peer(k)))

    barrier = pltpu.get_barrier_semaphore()
    for k in range(1, groups):
        pl.semaphore_signal(barrier, inc=1, device_id=group(peer(k)), device_id_type=MESH)
    for j in range(1, n_blk):
        pl.semaphore_signal(barrier, inc=1, device_id={"blk": lax.rem(b + j, n_blk)}, device_id_type=MESH)

    step_rows = 64

    @pl.loop(0, rows // step_rows)
    def _(t):
        at = pl.ds(pl.multiple_of(t * step_rows, step_rows), step_rows)
        x = emb[at, :]
        mean = jnp.sum(x * x, axis=1, keepdims=True) * (1.0 / features)
        inverse = lax.rsqrt(mean + epsilon) / jnp.sqrt(f32(features))
        normed[at, :] = (x * inverse).astype(bf16)

    member = lax.broadcasted_iota(jnp.int32, (1, rows), 1) < cnt_ref[...]
    cid = jnp.where(member, cid_ref[...], -1)
    onehot = lax.broadcasted_iota(jnp.int32, (groups, rows), 0) == cid
    onehot_f = jnp.where(onehot, 1.0, 0.0).astype(f32)
    below = lax.broadcasted_iota(jnp.int32, (rows, rows), 0) <= lax.broadcasted_iota(jnp.int32, (rows, rows), 1)
    upto = jnp.dot(
        onehot_f.astype(bf16), jnp.where(below, 1.0, 0.0).astype(bf16), preferred_element_type=f32
    )
    rank = jnp.sum(onehot_f * upto, axis=0, keepdims=True).astype(jnp.int32) - 1
    places = lax.broadcasted_iota(jnp.int32, (128, rows), 0)
    order = ord_ref[...]
    which = lax.broadcasted_iota(jnp.int32, (8, rows), 0)
    pieces = jnp.where(
        which == 0,
        order & 255,
        jnp.where(which == 1, (order >> 8) & 255, jnp.where(which == 2, order >> 16, 1)),
    )
    pieces = pieces.astype(f32).astype(bf16)

    pl.semaphore_wait(barrier, groups + n_blk - 2)

    def packed(c):
        choose = jnp.where(places == jnp.where(cid == c, rank, -1), 1.0, 0.0).astype(bf16)
        data = jnp.dot(choose[:capacity], normed[...], preferred_element_type=f32).astype(bf16)
        found = lax.dot_general(pieces, choose, NT, preferred_element_type=f32)
        value = (
            found[0:1] + 256.0 * found[1:2] + 65536.0 * found[2:3] + (1.0 - found[3:4]) * sentinel
        )
        return data, jnp.broadcast_to(value, (8, 128))

    @pl.loop(1, groups)
    def _(k):
        c = peer(k)
        data, value = packed(c)
        pack[block(c), :] = data
        order_out[c] = value
        rows_copy(k).start()
        order_copy(k).start()

    data, value = packed(g)
    got[b, block(g), :] = data
    order_in[b, g] = value

    def forward(k):
        core_copy(k).start()
        for m in range(1, chips):
            chip_copy(m, k).start()

    def relay(k):
        for m in range(1, chips):
            chip_copy(m, k).wait_recv()
            diagonal_copy(m, k).start()

    forward(0)

    @pl.loop(0, rows // step_rows)
    def _(t):
        at = pl.ds(pl.multiple_of(t * step_rows, step_rows), step_rows)
        x = emb[at, :]
        high = x.astype(bf16)
        emb_hi[at, :] = high
        emb_lo[at, :] = (x - high.astype(f32)).astype(bf16)

    for k in range(1, groups):
        order_copy(k).wait_recv()
    for j in range(1, n_blk):
        orders_copy(j).start()

    @pl.loop(1, groups)
    def _(k):
        rows_copy(k).wait_recv()
        forward(k)
        relay(k - 1)

    relay(groups - 1)

    def columns(j):
        for c in range(groups):
            flat = order_in[j, c].T
            order_col[j, c * capacity:(c + 1) * capacity, :] = jnp.broadcast_to(
                flat[:capacity, 0:1], (capacity, 128)
            )

    columns(b)
    order_row = order_col[b].T[0:1]
    half = slots // 2

    def scores(j, running):
        def one(t, running):
            at = pl.ds(pl.multiple_of(t * half, half), half)
            value = lax.dot_general(got[j, at, :], got[b], NT, preferred_element_type=f32)
            value = jnp.where(order_col[j, at, :][:, 0:1] < order_row, value, -1.0)
            return jnp.maximum(running, jnp.max(value.reshape(half // 8, 8, slots), axis=0))

        return lax.fori_loop(0, 2, one, running)

    running = scores(b, jnp.full((8, slots), -1.0, f32))
    for j in range(1, n_blk):
        orders_copy(j).wait_recv()
    for k in range(groups):
        core_copy(k).wait_recv()
    columns(other)
    running = scores(other, running)
    for m in range(1, chips):
        near = lax.rem(b + n_blk - 2 * m, n_blk)
        columns(near)
        running = scores(near, running)
        for k in range(groups):
            diagonal_copy(m, k).wait_recv()
        far = lax.rem(other + n_blk - 2 * m, n_blk)
        columns(far)
        running = scores(far, running)

    best = jnp.broadcast_to(jnp.max(running, axis=0, keepdims=True), (8, slots))
    for c in range(groups):
        shift = (slots - c * capacity) % slots
        home_out[c] = (pltpu.roll(best, shift, 1) if shift else best)[:, :128]
    for k in range(1, groups):
        home_copy(k).start()
    home_in[g] = home_out[g]
    for k in range(1, groups):
        home_copy(k).wait_recv()

    home = home_in[:, 0, :]
    h1 = home.astype(bf16).astype(f32)
    h2 = (home - h1).astype(bf16).astype(f32)
    h3 = home - h1 - h2
    spread = jnp.where(places == rank, 1.0, 0.0).astype(bf16)
    stack = jnp.concatenate([h1, h2, h3, jnp.zeros_like(h1)], axis=0).astype(bf16)
    table = jnp.dot(stack, spread, preferred_element_type=f32)
    table = table[:groups] + table[groups:2 * groups] + table[2 * groups:3 * groups]
    best_row = jnp.sum(onehot_f * table, axis=0, keepdims=True)
    best_ref[...] = best_row
    keep = onehot_f * (1.0 / (1.0 + jnp.exp(-10.0 * (0.5 - best_row))))
    k1 = keep.astype(bf16).astype(f32)
    both = jnp.concatenate([k1, keep - k1], axis=0).astype(bf16)
    sums = jnp.dot(both, emb_hi[...], preferred_element_type=f32) + jnp.dot(
        both, emb_lo[...], preferred_element_type=f32
    )
    sums = sums[:groups] + sums[groups:]
    weight = jnp.sum(keep, axis=1, keepdims=True)
    width = features // n_blk
    for j in range(n_blk):
        part[j, :, :width] = sums[:, j * width:(j + 1) * width]
        part[j, :, width:] = jnp.broadcast_to(weight, (groups, 128))
    for j in range(1, n_blk):
        part_copy(j).start()
    part_in[b] = part[b]
    for j in range(1, n_blk):
        part_copy(j).wait_recv()
    total = part_in[0]
    for j in range(1, n_blk):
        total = total + part_in[j]
    for c in range(groups):
        row_out[c] = jnp.broadcast_to(total[c:c + 1], (8, width + 128))
    for k in range(1, groups):
        row_copy(k).start()
    row_in[g] = row_out[g]
    for k in range(1, groups):
        row_copy(k).wait_recv()
    final = jnp.sum(row_in[...], axis=0)
    cent_ref[...] = final[0:1, :width] / jnp.sqrt(1.0 + final[0:1, width:width + 1])

    for k in range(groups):
        core_copy(k).wait_send()
        for m in range(1, chips):
            chip_copy(m, k).wait_send()
            diagonal_copy(m, k).wait_send()
    for k in range(1, groups):
        rows_copy(k).wait_send()
        order_copy(k).wait_send()
        home_copy(k).wait_send()
        row_copy(k).wait_send()
    for j in range(1, n_blk):
        orders_copy(j).wait_send()
        part_copy(j).wait_send()


def solution(mesh):
    n_dp, n_blk, n_cent = (mesh.shape[name] for name in ("dp", "blk", "cent"))
    groups = n_dp * n_cent

    def on_device(embeddings, cluster_ids, order_index, shard_counts):
        rows, features = embeddings.shape
        capacity = 3 * rows // (2 * groups)
        capacity = (capacity + 15) // 16 * 16
        slots = groups * capacity
        width = features // n_blk
        f32, bf16 = jnp.float32, jnp.bfloat16
        sem = pltpu.SemaphoreType.DMA
        chips = n_blk // 2
        best, centroid = pl.pallas_call(
            functools.partial(kernel, n_dp, n_blk, n_cent, capacity),
            out_shape=(
                jax.ShapeDtypeStruct((1, rows), f32),
                jax.ShapeDtypeStruct((1, width), f32),
            ),
            in_specs=[pl.BlockSpec(memory_space=pltpu.VMEM)] * 4,
            out_specs=(pl.BlockSpec(memory_space=pltpu.VMEM),) * 2,
            scratch_shapes=[
                pltpu.VMEM((rows, features), bf16),
                pltpu.VMEM((rows, features), bf16),
                pltpu.VMEM((rows, features), bf16),
                pltpu.VMEM((slots, features), bf16),
                pltpu.VMEM((n_blk, slots, features), bf16),
                pltpu.VMEM((groups, 8, 128), f32),
                pltpu.VMEM((n_blk, groups, 8, 128), f32),
                pltpu.VMEM((n_blk, slots, 128), f32),
                pltpu.VMEM((groups, 8, 128), f32),
                pltpu.VMEM((groups, 8, 128), f32),
                pltpu.VMEM((n_blk, groups, width + 128), f32),
                pltpu.VMEM((n_blk, groups, width + 128), f32),
                pltpu.VMEM((groups, 8, width + 128), f32),
                pltpu.VMEM((groups, 8, width + 128), f32),
                sem((groups,)), sem((groups,)), sem((groups,)), sem((groups,)),
                sem((groups,)), sem((groups,)),
                sem((chips, groups)), sem((chips, groups)),
                sem((chips, groups)), sem((chips, groups)),
                sem((n_blk,)), sem((n_blk,)),
                sem((groups,)), sem((groups,)),
                sem((n_blk,)), sem((n_blk,)),
                sem((groups,)), sem((groups,)),
            ],
            compiler_params=pltpu.CompilerParams(
                collective_id=0, has_side_effects=True, vmem_limit_bytes=48 * 1024 * 1024
            ),
        )(
            embeddings,
            cluster_ids.reshape(1, rows),
            order_index.reshape(1, rows),
            shard_counts.reshape(1, 1),
        )
        return best.reshape(rows), centroid

    placed = (
        P(("dp", "blk", "cent"), None),
        P(("dp", "blk", "cent"), None),
        P(("dp", "blk", "cent")),
        P(("dp", "blk", "cent")),
    )
    return jax.shard_map(
        on_device,
        mesh=mesh,
        in_specs=placed,
        out_specs=(P(("dp", "blk", "cent")), P(("dp", "cent"), "blk")),
        check_vma=False,
    )
```

```python
import functools

import jax
import jax.numpy as jnp
from jax import lax
from jax.experimental import pallas as pl
from jax.experimental.pallas import tpu as pltpu
from jax.sharding import PartitionSpec as P

epsilon = 1e-06
sentinel = 1073741824.0
MESH = pl.DeviceIdType.MESH
NT = (((1,), (1,)), ((), ()))


def kernel(
    n_dp, n_blk, n_cent, capacity,
    emb, cid_ref, ord_ref, cnt_ref,
    best_ref, cent_ref,
    normed, emb_hi, emb_lo, pack, got, order_out, order_in, order_col,
    home_out, home_in, part, part_in, row_out, row_in,
    a_send, a_recv, o_send, o_recv, c_send, c_recv, y_send, y_recv, d_send, d_recv,
    p_send, p_recv, h_send, h_recv, r_send, r_recv, s_send, s_recv,
):
    groups = n_dp * n_cent
    rows, features = emb.shape
    slots = groups * capacity
    b = lax.axis_index("blk")
    g = lax.axis_index("dp") * n_cent + lax.axis_index("cent")
    chips = n_blk // 2
    pieces_per = 2 if capacity % 32 == 0 else 1
    size = capacity // pieces_per
    other = b + 1 - 2 * lax.rem(b, 2)
    f32, bf16 = jnp.float32, jnp.bfloat16

    def group(index):
        return {"dp": index // n_cent, "cent": lax.rem(index, n_cent)}

    def peer(k):
        result, bit = g, 1
        while bit < groups:
            if (k // bit) % 2:
                result = result + bit - 2 * bit * lax.rem(g // bit, 2)
            bit *= 2
        return result

    def block(index):
        return pl.ds(pl.multiple_of(index * capacity, capacity), capacity)

    def piece(index, h):
        return pl.ds(pl.multiple_of(index * capacity + h * size, size), size)

    def remote(src, dst, send, recv, device):
        return pltpu.make_async_remote_copy(
            src_ref=src, dst_ref=dst, send_sem=send, recv_sem=recv,
            device_id=device, device_id_type=MESH,
        )

    def rows_copy(k, h):
        return remote(
            pack.at[piece(peer(k), h)], got.at[b, piece(g, h)], a_send.at[k, h], a_recv.at[k, h], group(peer(k))
        )

    def order_copy(k):
        return remote(order_out.at[peer(k)], order_in.at[b, g], o_send.at[k], o_recv.at[k], group(peer(k)))

    def core_copy(k, h):
        part_of = got.at[b, piece(peer(k), h)]
        return remote(part_of, part_of, c_send.at[k, h], c_recv.at[k, h], {"blk": other})

    def chip_copy(m, k, h):
        part_of = got.at[b, piece(peer(k), h)]
        return remote(
            part_of, part_of, y_send.at[m, k, h], y_recv.at[m, k, h], {"blk": lax.rem(b + 2 * m, n_blk)}
        )

    def diagonal_copy(m, k, h):
        part_of = got.at[lax.rem(b + n_blk - 2 * m, n_blk), piece(peer(k), h)]
        return remote(part_of, part_of, d_send.at[m, k, h], d_recv.at[m, k, h], {"blk": other})

    def orders_copy(j):
        return remote(order_in.at[b], order_in.at[b], p_send.at[j], p_recv.at[j], {"blk": lax.rem(b + j, n_blk)})

    def home_copy(k):
        return remote(home_out.at[peer(k)], home_in.at[g], h_send.at[k], h_recv.at[k], group(peer(k)))

    def part_copy(j):
        return remote(
            part.at[lax.rem(b + j, n_blk)], part_in.at[b], r_send.at[j], r_recv.at[j], {"blk": lax.rem(b + j, n_blk)}
        )

    def row_copy(k):
        return remote(row_out.at[peer(k)], row_in.at[g], s_send.at[k], s_recv.at[k], group(peer(k)))

    barrier = pltpu.get_barrier_semaphore()
    for k in range(1, groups):
        pl.semaphore_signal(barrier, inc=1, device_id=group(peer(k)), device_id_type=MESH)
    for j in range(1, n_blk):
        pl.semaphore_signal(barrier, inc=1, device_id={"blk": lax.rem(b + j, n_blk)}, device_id_type=MESH)

    step_rows = 64

    @pl.loop(0, rows // step_rows)
    def _(t):
        at = pl.ds(pl.multiple_of(t * step_rows, step_rows), step_rows)
        x = emb[at, :]
        mean = jnp.sum(x * x, axis=1, keepdims=True) * (1.0 / features)
        inverse = lax.rsqrt(mean + epsilon) / jnp.sqrt(f32(features))
        normed[at, :] = (x * inverse).astype(bf16)

    member = lax.broadcasted_iota(jnp.int32, (1, rows), 1) < cnt_ref[...]
    cid = jnp.where(member, cid_ref[...], -1)
    onehot = lax.broadcasted_iota(jnp.int32, (groups, rows), 0) == cid
    onehot_f = jnp.where(onehot, 1.0, 0.0).astype(f32)
    below = lax.broadcasted_iota(jnp.int32, (rows, rows), 0) <= lax.broadcasted_iota(jnp.int32, (rows, rows), 1)
    upto = jnp.dot(
        onehot_f.astype(bf16), jnp.where(below, 1.0, 0.0).astype(bf16), preferred_element_type=f32
    )
    rank = jnp.sum(onehot_f * upto, axis=0, keepdims=True).astype(jnp.int32) - 1
    places = lax.broadcasted_iota(jnp.int32, (128, rows), 0)
    order = ord_ref[...]
    which = lax.broadcasted_iota(jnp.int32, (8, rows), 0)
    pieces = jnp.where(
        which == 0,
        order & 255,
        jnp.where(which == 1, (order >> 8) & 255, jnp.where(which == 2, order >> 16, 1)),
    )
    pieces = pieces.astype(f32).astype(bf16)

    pl.semaphore_wait(barrier, groups + n_blk - 2)

    def packed(c):
        choose = jnp.where(places == jnp.where(cid == c, rank, -1), 1.0, 0.0).astype(bf16)
        data = jnp.dot(choose[:capacity], normed[...], preferred_element_type=f32).astype(bf16)
        found = lax.dot_general(pieces, choose, NT, preferred_element_type=f32)
        value = (
            found[0:1] + 256.0 * found[1:2] + 65536.0 * found[2:3] + (1.0 - found[3:4]) * sentinel
        )
        return data, jnp.broadcast_to(value, (8, 128))

    span = max(n_cent // 2, 1)
    far_ones = [k for k in range(1, groups) if (k % n_cent) >= span]
    near_ones = [k for k in range(1, groups) if (k % n_cent) < span]
    near_ones.sort(key=lambda k: (k % n_cent) + (k // n_cent) * (k % n_cent > 0) * n_cent)
    far_units = [(k, h) for k in far_ones for h in range(pieces_per)]
    near_units = [(k, h) for k in near_ones for h in range(pieces_per)]
    arrival = [(2 * i + 2.5, u) for i, u in enumerate(far_units)]
    arrival += [(i + 1, u) for i, u in enumerate(near_units)]
    arrival = [u for _, u in sorted(arrival)]
    window = 3
    waiting = far_units[window:]

    def forward(k, h):
        core_copy(k, h).start()
        for m in range(1, chips):
            chip_copy(m, k, h).start()

    def relay(k, h):
        for m in range(1, chips):
            chip_copy(m, k, h).wait_recv()
            diagonal_copy(m, k, h).start()

    def prepare(k):
        c = peer(k)
        data, value = packed(c)
        pack[block(c), :] = data
        order_out[c] = value
        order_copy(k).start()
        for h in range(pieces_per):
            if (k, h) not in waiting:
                rows_copy(k, h).start()

    prepare(far_ones[0])
    for k in near_ones[:1]:
        prepare(k)
    data, value = packed(g)
    got[b, block(g), :] = data
    order_in[b, g] = value
    for h in range(pieces_per):
        forward(0, h)
    for k in near_ones[1:] + far_ones[1:]:
        prepare(k)

    done = [(0, h) for h in range(pieces_per)]
    lag = 2
    relayed = 0
    for at_unit in arrival:
        rows_copy(*at_unit).wait_recv()
        if at_unit in far_units and waiting:
            rows_copy(*waiting.pop(0)).start()
        forward(*at_unit)
        done.append(at_unit)
        while relayed < len(done) - lag:
            relay(*done[relayed])
            relayed += 1

    for k in range(1, groups):
        order_copy(k).wait_recv()
    for j in range(1, n_blk):
        orders_copy(j).start()

    @pl.loop(0, rows // step_rows)
    def _(t):
        at = pl.ds(pl.multiple_of(t * step_rows, step_rows), step_rows)
        x = emb[at, :]
        high = x.astype(bf16)
        emb_hi[at, :] = high
        emb_lo[at, :] = (x - high.astype(f32)).astype(bf16)

    def columns(j):
        for c in range(groups):
            flat = order_in[j, c].T
            order_col[j, c * capacity:(c + 1) * capacity, :] = jnp.broadcast_to(
                flat[:capacity, 0:1], (capacity, 128)
            )

    columns(b)
    order_row = order_col[b].T[0:1]
    half = slots // 2

    def scores(j, running):
        def one(t, running):
            at = pl.ds(pl.multiple_of(t * half, half), half)
            value = lax.dot_general(got[j, at, :], got[b], NT, preferred_element_type=f32)
            value = jnp.where(order_col[j, at, :][:, 0:1] < order_row, value, -1.0)
            return jnp.maximum(running, jnp.max(value.reshape(half // 8, 8, slots), axis=0))

        return lax.fori_loop(0, 2, one, running)

    running = scores(b, jnp.full((8, slots), -1.0, f32))
    for unit in done[relayed:]:
        relay(*unit)
    for j in range(1, n_blk):
        orders_copy(j).wait_recv()
    for unit in done:
        core_copy(*unit).wait_recv()
    columns(other)
    running = scores(other, running)
    for m in range(1, chips):
        near = lax.rem(b + n_blk - 2 * m, n_blk)
        columns(near)
        running = scores(near, running)
        for unit in done:
            diagonal_copy(m, *unit).wait_recv()
        far = lax.rem(other + n_blk - 2 * m, n_blk)
        columns(far)
        running = scores(far, running)

    best = jnp.broadcast_to(jnp.max(running, axis=0, keepdims=True), (8, slots))
    for c in range(groups):
        shift = (slots - c * capacity) % slots
        home_out[c] = (pltpu.roll(best, shift, 1) if shift else best)[:, :128]
    for k in range(1, groups):
        home_copy(k).start()
    home_in[g] = home_out[g]
    for k in range(1, groups):
        home_copy(k).wait_recv()

    home = home_in[:, 0, :]
    h1 = home.astype(bf16).astype(f32)
    h2 = (home - h1).astype(bf16).astype(f32)
    h3 = home - h1 - h2
    spread = jnp.where(places == rank, 1.0, 0.0).astype(bf16)
    stack = jnp.concatenate([h1, h2, h3, jnp.zeros_like(h1)], axis=0).astype(bf16)
    table = jnp.dot(stack, spread, preferred_element_type=f32)
    table = table[:groups] + table[groups:2 * groups] + table[2 * groups:3 * groups]
    best_row = jnp.sum(onehot_f * table, axis=0, keepdims=True)
    best_ref[...] = best_row
    keep = onehot_f * (1.0 / (1.0 + jnp.exp(-10.0 * (0.5 - best_row))))
    k1 = keep.astype(bf16).astype(f32)
    both = jnp.concatenate([k1, keep - k1], axis=0).astype(bf16)
    sums = jnp.dot(both, emb_hi[...], preferred_element_type=f32) + jnp.dot(
        both, emb_lo[...], preferred_element_type=f32
    )
    sums = sums[:groups] + sums[groups:]
    weight = jnp.sum(keep, axis=1, keepdims=True)
    width = features // n_blk
    for j in range(n_blk):
        part[j, :, :width] = sums[:, j * width:(j + 1) * width]
        part[j, :, width:] = jnp.broadcast_to(weight, (groups, 128))
    for j in range(1, n_blk):
        part_copy(j).start()
    part_in[b] = part[b]
    for j in range(1, n_blk):
        part_copy(j).wait_recv()
    total = part_in[0]
    for j in range(1, n_blk):
        total = total + part_in[j]
    for c in range(groups):
        row_out[c] = jnp.broadcast_to(total[c:c + 1], (8, width + 128))
    for k in range(1, groups):
        row_copy(k).start()
    row_in[g] = row_out[g]
    for k in range(1, groups):
        row_copy(k).wait_recv()
    final = jnp.sum(row_in[...], axis=0)
    cent_ref[...] = final[0:1, :width] / jnp.sqrt(1.0 + final[0:1, width:width + 1])

    for unit in done:
        core_copy(*unit).wait_send()
        for m in range(1, chips):
            chip_copy(m, *unit).wait_send()
            diagonal_copy(m, *unit).wait_send()
    for unit in arrival:
        rows_copy(*unit).wait_send()
    for k in range(1, groups):
        order_copy(k).wait_send()
        home_copy(k).wait_send()
        row_copy(k).wait_send()
    for j in range(1, n_blk):
        orders_copy(j).wait_send()
        part_copy(j).wait_send()


def solution(mesh):
    n_dp, n_blk, n_cent = (mesh.shape[name] for name in ("dp", "blk", "cent"))
    groups = n_dp * n_cent

    def on_device(embeddings, cluster_ids, order_index, shard_counts):
        rows, features = embeddings.shape
        capacity = 3 * rows // (2 * groups)
        capacity = (capacity + 15) // 16 * 16
        slots = groups * capacity
        width = features // n_blk
        f32, bf16 = jnp.float32, jnp.bfloat16
        sem = pltpu.SemaphoreType.DMA
        chips = n_blk // 2
        best, centroid = pl.pallas_call(
            functools.partial(kernel, n_dp, n_blk, n_cent, capacity),
            out_shape=(
                jax.ShapeDtypeStruct((1, rows), f32),
                jax.ShapeDtypeStruct((1, width), f32),
            ),
            in_specs=[pl.BlockSpec(memory_space=pltpu.VMEM)] * 4,
            out_specs=(pl.BlockSpec(memory_space=pltpu.VMEM),) * 2,
            scratch_shapes=[
                pltpu.VMEM((rows, features), bf16),
                pltpu.VMEM((rows, features), bf16),
                pltpu.VMEM((rows, features), bf16),
                pltpu.VMEM((slots, features), bf16),
                pltpu.VMEM((n_blk, slots, features), bf16),
                pltpu.VMEM((groups, 8, 128), f32),
                pltpu.VMEM((n_blk, groups, 8, 128), f32),
                pltpu.VMEM((n_blk, slots, 128), f32),
                pltpu.VMEM((groups, 8, 128), f32),
                pltpu.VMEM((groups, 8, 128), f32),
                pltpu.VMEM((n_blk, groups, width + 128), f32),
                pltpu.VMEM((n_blk, groups, width + 128), f32),
                pltpu.VMEM((groups, 8, width + 128), f32),
                pltpu.VMEM((groups, 8, width + 128), f32),
                sem((groups, 2)), sem((groups, 2)), sem((groups,)), sem((groups,)),
                sem((groups, 2)), sem((groups, 2)),
                sem((chips, groups, 2)), sem((chips, groups, 2)),
                sem((chips, groups, 2)), sem((chips, groups, 2)),
                sem((n_blk,)), sem((n_blk,)),
                sem((groups,)), sem((groups,)),
                sem((n_blk,)), sem((n_blk,)),
                sem((groups,)), sem((groups,)),
            ],
            compiler_params=pltpu.CompilerParams(
                collective_id=0, has_side_effects=True, vmem_limit_bytes=48 * 1024 * 1024
            ),
        )(
            embeddings,
            cluster_ids.reshape(1, rows),
            order_index.reshape(1, rows),
            shard_counts.reshape(1, 1),
        )
        return best.reshape(rows), centroid

    placed = (
        P(("dp", "blk", "cent"), None),
        P(("dp", "blk", "cent"), None),
        P(("dp", "blk", "cent")),
        P(("dp", "blk", "cent")),
    )
    return jax.shard_map(
        on_device,
        mesh=mesh,
        in_specs=placed,
        out_specs=(P(("dp", "blk", "cent")), P(("dp", "cent"), "blk")),
        check_vma=False,
    )
```

```python
import functools

import jax
import jax.numpy as jnp
from jax import lax
from jax.experimental import pallas as pl
from jax.experimental.pallas import tpu as pltpu
from jax.sharding import PartitionSpec as P

epsilon = 1e-06
sentinel = 1073741824.0
MESH = pl.DeviceIdType.MESH
NT = (((1,), (1,)), ((), ()))


def kernel(
    n_dp, n_blk, n_cent, capacity,
    emb_any, cid_any, ord_any, cnt_ref,
    best_ref, cent_ref,
    emb, cid_ref, ord_ref, in_sem, normed, emb_hi, emb_lo, pack, got, order_out, order_in, order_col,
    home_out, home_in, part, part_in, row_out, row_in,
    a_send, a_recv, o_send, o_recv, c_send, c_recv, y_send, y_recv, d_send, d_recv,
    p_send, p_recv, h_send, h_recv, r_send, r_recv, s_send, s_recv,
):
    groups = n_dp * n_cent
    rows, features = emb_any.shape
    slots = groups * capacity
    b = lax.axis_index("blk")
    g = lax.axis_index("dp") * n_cent + lax.axis_index("cent")
    chips = n_blk // 2
    pieces_per = 2 if capacity % 32 == 0 else 1
    size = capacity // pieces_per
    other = b + 1 - 2 * lax.rem(b, 2)
    f32, bf16 = jnp.float32, jnp.bfloat16

    def group(index):
        return {"dp": index // n_cent, "cent": lax.rem(index, n_cent)}

    def peer(k):
        result, bit = g, 1
        while bit < groups:
            if (k // bit) % 2:
                result = result + bit - 2 * bit * lax.rem(g // bit, 2)
            bit *= 2
        return result

    def block(index):
        return pl.ds(pl.multiple_of(index * capacity, capacity), capacity)

    def piece(index, h):
        return pl.ds(pl.multiple_of(index * capacity + h * size, size), size)

    def remote(src, dst, send, recv, device):
        return pltpu.make_async_remote_copy(
            src_ref=src, dst_ref=dst, send_sem=send, recv_sem=recv,
            device_id=device, device_id_type=MESH,
        )

    span = max(n_cent // 2, 1)
    far_ones = [k for k in range(1, groups) if (k % n_cent) >= span]
    near_ones = [k for k in range(1, groups) if (k % n_cent) < span]
    near_ones.sort(key=lambda k: (k % n_cent) + (k // n_cent) * (k % n_cent > 0) * n_cent)
    far_units = [(k, h) for k in far_ones for h in range(pieces_per)]
    near_units = [(k, h) for k in near_ones for h in range(pieces_per)]
    arrival = [(2 * i + 2.5, u) for i, u in enumerate(far_units)]
    arrival += [(i + 1, u) for i, u in enumerate(near_units)]
    arrival = [u for _, u in sorted(arrival)]
    position = {0: 0}
    for k, h in arrival:
        if h == pieces_per - 1:
            position[k] = len(position)

    def rows_copy(k, h):
        return remote(
            pack.at[piece(peer(k), h)], got.at[b, piece(position[k], h)], a_send.at[k, h], a_recv.at[k, h], group(peer(k))
        )

    def order_copy(k):
        return remote(order_out.at[peer(k)], order_in.at[b, position[k]], o_send.at[k], o_recv.at[k], group(peer(k)))

    def core_copy(k, h):
        part_of = got.at[b, piece(position[k], h)]
        return remote(part_of, part_of, c_send.at[k, h], c_recv.at[k, h], {"blk": other})

    def chip_copy(m, k, h):
        part_of = got.at[b, piece(position[k], h)]
        return remote(
            part_of, part_of, y_send.at[m, k, h], y_recv.at[m, k, h], {"blk": lax.rem(b + 2 * m, n_blk)}
        )

    def diagonal_copy(m, k, h):
        part_of = got.at[lax.rem(b + n_blk - 2 * m, n_blk), piece(position[k], h)]
        return remote(part_of, part_of, d_send.at[m, k, h], d_recv.at[m, k, h], {"blk": other})

    def orders_copy(j):
        return remote(order_in.at[b], order_in.at[b], p_send.at[j], p_recv.at[j], {"blk": lax.rem(b + j, n_blk)})

    def home_copy(k):
        return remote(home_out.at[position[k]], home_in.at[g], h_send.at[k], h_recv.at[k], group(peer(k)))

    def part_copy(j):
        return remote(
            part.at[lax.rem(b + j, n_blk)], part_in.at[b], r_send.at[j], r_recv.at[j], {"blk": lax.rem(b + j, n_blk)}
        )

    def row_copy(k):
        return remote(row_out.at[peer(k)], row_in.at[g], s_send.at[k], s_recv.at[k], group(peer(k)))

    step_rows = 64
    steps = rows // step_rows

    def chunk(t):
        return pl.ds(pl.multiple_of(t * step_rows, step_rows), step_rows)

    def load(t):
        return pltpu.make_async_copy(emb_any.at[chunk(t)], emb.at[chunk(t)], in_sem.at[t])

    load_cid = pltpu.make_async_copy(cid_any, cid_ref, in_sem.at[steps])
    load_ord = pltpu.make_async_copy(ord_any, ord_ref, in_sem.at[steps + 1])
    load_cid.start()
    load_ord.start()
    for t in range(steps):
        load(t).start()

    barrier = pltpu.get_barrier_semaphore()
    for k in range(1, groups):
        pl.semaphore_signal(barrier, inc=1, device_id=group(peer(k)), device_id_type=MESH)
    for j in range(1, n_blk):
        pl.semaphore_signal(barrier, inc=1, device_id={"blk": lax.rem(b + j, n_blk)}, device_id_type=MESH)

    load_cid.wait()
    load_ord.wait()
    member = lax.broadcasted_iota(jnp.int32, (1, rows), 1) < cnt_ref[...]
    cid = jnp.where(member, cid_ref[...], -1)
    onehot = lax.broadcasted_iota(jnp.int32, (groups, rows), 0) == cid
    onehot_f = jnp.where(onehot, 1.0, 0.0).astype(f32)
    below = lax.broadcasted_iota(jnp.int32, (rows, rows), 0) <= lax.broadcasted_iota(jnp.int32, (rows, rows), 1)
    upto = jnp.dot(
        onehot_f.astype(bf16), jnp.where(below, 1.0, 0.0).astype(bf16), preferred_element_type=f32
    )
    rank = jnp.sum(onehot_f * upto, axis=0, keepdims=True).astype(jnp.int32) - 1
    places = lax.broadcasted_iota(jnp.int32, (128, rows), 0)
    order = ord_ref[...]
    which = lax.broadcasted_iota(jnp.int32, (8, rows), 0)
    pieces = jnp.where(
        which == 0,
        order & 255,
        jnp.where(which == 1, (order >> 8) & 255, jnp.where(which == 2, order >> 16, 1)),
    )
    pieces = pieces.astype(f32).astype(bf16)

    @pl.loop(0, steps)
    def _(t):
        load(t).wait()
        at = chunk(t)
        x = emb[at, :]
        mean = jnp.sum(x * x, axis=1, keepdims=True) * (1.0 / features)
        inverse = lax.rsqrt(mean + epsilon) / jnp.sqrt(f32(features))
        normed[at, :] = (x * inverse).astype(bf16)

    pl.semaphore_wait(barrier, groups + n_blk - 2)

    def packed(c):
        choose = jnp.where(places == jnp.where(cid == c, rank, -1), 1.0, 0.0).astype(bf16)
        data = jnp.dot(choose[:capacity], normed[...], preferred_element_type=f32).astype(bf16)
        found = lax.dot_general(pieces, choose, NT, preferred_element_type=f32)
        value = (
            found[0:1] + 256.0 * found[1:2] + 65536.0 * found[2:3] + (1.0 - found[3:4]) * sentinel
        )
        return data, jnp.broadcast_to(value, (8, 128))

    window = 3
    waiting = far_units[window:]

    def forward(k, h):
        core_copy(k, h).start()
        for m in range(1, chips):
            chip_copy(m, k, h).start()

    def relay(k, h):
        for m in range(1, chips):
            chip_copy(m, k, h).wait_recv()
            diagonal_copy(m, k, h).start()

    def prepare(k):
        c = peer(k)
        data, value = packed(c)
        pack[block(c), :] = data
        order_out[c] = value
        order_copy(k).start()
        for h in range(pieces_per):
            if (k, h) not in waiting:
                rows_copy(k, h).start()

    prepare(far_ones[0])
    for k in near_ones[:1]:
        prepare(k)
    data, value = packed(g)
    got[b, :capacity, :] = data
    order_in[b, 0] = value
    for h in range(pieces_per):
        forward(0, h)
    for k in near_ones[1:] + far_ones[1:]:
        prepare(k)

    @pl.loop(0, steps)
    def _(t):
        at = chunk(t)
        x = emb[at, :]
        high = x.astype(bf16)
        emb_hi[at, :] = high
        emb_lo[at, :] = (x - high.astype(f32)).astype(bf16)

    def columns(j):
        for c in range(groups):
            flat = order_in[j, c].T
            order_col[j, c * capacity:(c + 1) * capacity, :] = jnp.broadcast_to(
                flat[:capacity, 0:1], (capacity, 128)
            )

    done = [(0, h) for h in range(pieces_per)]
    lag = 3
    relayed = 0
    for number, at_unit in enumerate(arrival):
        if number == len(arrival) // 2:
            for k in range(1, groups):
                order_copy(k).wait_recv()
            for j in range(1, n_blk):
                orders_copy(j).start()
            columns(b)
        if number == len(arrival) - 2:
            for j in range(1, n_blk):
                orders_copy(j).wait_recv()
                columns(lax.rem(b + n_blk - j, n_blk))
        rows_copy(*at_unit).wait_recv()
        if at_unit in far_units and waiting:
            rows_copy(*waiting.pop(0)).start()
        forward(*at_unit)
        done.append(at_unit)
        while relayed < len(done) - lag:
            relay(*done[relayed])
            relayed += 1

    order_row = order_col[b].T[0:1]
    half = slots // 2

    def scores(j, t, running):
        at = pl.ds(t * half if isinstance(t, int) else pl.multiple_of(t * half, half), half)
        value = lax.dot_general(got[j, at, :], got[b], NT, preferred_element_type=f32)
        value = jnp.where(order_col[j, at, :][:, 0:1] < order_row, value, -1.0)
        return jnp.maximum(running, jnp.max(value.reshape(half // 8, 8, slots), axis=0))

    def both(j, running):
        return lax.fori_loop(0, 2, lambda t, r: scores(j, t, r), running)

    first = [u for u in done if position[u[0]] < groups // 2]
    second = [u for u in done if position[u[0]] >= groups // 2]

    def relay_upto(count):
        nonlocal relayed
        while relayed < min(count, len(done)):
            relay(*done[relayed])
            relayed += 1

    running = both(b, jnp.full((8, slots), -1.0, f32))
    relay_upto(len(done) - 2)
    for unit in done:
        core_copy(*unit).wait_recv()
    running = both(other, running)
    for number, (units, t) in enumerate(((first, 0), (second, 1))):
        if number == 1:
            relay_upto(len(done))
        for m in range(1, chips):
            running = scores(lax.rem(b + n_blk - 2 * m, n_blk), t, running)
            for unit in units:
                diagonal_copy(m, *unit).wait_recv()
            running = scores(lax.rem(other + n_blk - 2 * m, n_blk), t, running)

    best = jnp.broadcast_to(jnp.max(running, axis=0, keepdims=True), (8, slots))
    for c in range(groups):
        shift = (slots - c * capacity) % slots
        home_out[c] = (pltpu.roll(best, shift, 1) if shift else best)[:, :128]
    for k in range(1, groups):
        home_copy(k).start()
    home_in[g] = home_out[0]
    for k in range(1, groups):
        home_copy(k).wait_recv()

    home = home_in[:, 0, :]
    h1 = home.astype(bf16).astype(f32)
    h2 = (home - h1).astype(bf16).astype(f32)
    h3 = home - h1 - h2
    spread = jnp.where(places == rank, 1.0, 0.0).astype(bf16)
    stack = jnp.concatenate([h1, h2, h3, jnp.zeros_like(h1)], axis=0).astype(bf16)
    table = jnp.dot(stack, spread, preferred_element_type=f32)
    table = table[:groups] + table[groups:2 * groups] + table[2 * groups:3 * groups]
    best_row = jnp.sum(onehot_f * table, axis=0, keepdims=True)
    best_ref[...] = best_row
    keep = onehot_f * (1.0 / (1.0 + jnp.exp(-10.0 * (0.5 - best_row))))
    k1 = keep.astype(bf16).astype(f32)
    pair = jnp.concatenate([k1, keep - k1], axis=0).astype(bf16)
    sums = jnp.dot(pair, emb_hi[...], preferred_element_type=f32) + jnp.dot(
        pair, emb_lo[...], preferred_element_type=f32
    )
    sums = sums[:groups] + sums[groups:]
    weight = jnp.sum(keep, axis=1, keepdims=True)
    width = features // n_blk
    for j in range(n_blk):
        part[j, :, :width] = sums[:, j * width:(j + 1) * width]
        part[j, :, width:] = jnp.broadcast_to(weight, (groups, 128))
    for j in range(1, n_blk):
        part_copy(j).start()
    part_in[b] = part[b]
    for j in range(1, n_blk):
        part_copy(j).wait_recv()
    total = part_in[0]
    for j in range(1, n_blk):
        total = total + part_in[j]
    for c in range(groups):
        row_out[c] = jnp.broadcast_to(total[c:c + 1], (8, width + 128))
    for k in range(1, groups):
        row_copy(k).start()
    row_in[g] = row_out[g]
    for k in range(1, groups):
        row_copy(k).wait_recv()
    final = jnp.sum(row_in[...], axis=0)
    cent_ref[...] = final[0:1, :width] / jnp.sqrt(1.0 + final[0:1, width:width + 1])

    for unit in done:
        core_copy(*unit).wait_send()
        for m in range(1, chips):
            chip_copy(m, *unit).wait_send()
            diagonal_copy(m, *unit).wait_send()
    for unit in arrival:
        rows_copy(*unit).wait_send()
    for k in range(1, groups):
        order_copy(k).wait_send()
        home_copy(k).wait_send()
        row_copy(k).wait_send()
    for j in range(1, n_blk):
        orders_copy(j).wait_send()
        part_copy(j).wait_send()


def solution(mesh):
    n_dp, n_blk, n_cent = (mesh.shape[name] for name in ("dp", "blk", "cent"))
    groups = n_dp * n_cent

    def on_device(embeddings, cluster_ids, order_index, shard_counts):
        rows, features = embeddings.shape
        capacity = 3 * rows // (2 * groups)
        capacity = (capacity + 15) // 16 * 16
        slots = groups * capacity
        width = features // n_blk
        f32, bf16 = jnp.float32, jnp.bfloat16
        sem = pltpu.SemaphoreType.DMA
        chips = n_blk // 2
        best, centroid = pl.pallas_call(
            functools.partial(kernel, n_dp, n_blk, n_cent, capacity),
            out_shape=(
                jax.ShapeDtypeStruct((1, rows), f32),
                jax.ShapeDtypeStruct((1, width), f32),
            ),
            in_specs=[pl.BlockSpec(memory_space=pl.ANY)] * 3 + [pl.BlockSpec(memory_space=pltpu.VMEM)],
            out_specs=(pl.BlockSpec(memory_space=pltpu.VMEM),) * 2,
            scratch_shapes=[
                pltpu.VMEM((rows, features), f32),
                pltpu.VMEM((1, rows), jnp.int32),
                pltpu.VMEM((1, rows), jnp.int32),
                sem((rows // 64 + 2,)),
                pltpu.VMEM((rows, features), bf16),
                pltpu.VMEM((rows, features), bf16),
                pltpu.VMEM((rows, features), bf16),
                pltpu.VMEM((slots, features), bf16),
                pltpu.VMEM((n_blk, slots, features), bf16),
                pltpu.VMEM((groups, 8, 128), f32),
                pltpu.VMEM((n_blk, groups, 8, 128), f32),
                pltpu.VMEM((n_blk, slots, 128), f32),
                pltpu.VMEM((groups, 8, 128), f32),
                pltpu.VMEM((groups, 8, 128), f32),
                pltpu.VMEM((n_blk, groups, width + 128), f32),
                pltpu.VMEM((n_blk, groups, width + 128), f32),
                pltpu.VMEM((groups, 8, width + 128), f32),
                pltpu.VMEM((groups, 8, width + 128), f32),
                sem((groups, 2)), sem((groups, 2)), sem((groups,)), sem((groups,)),
                sem((groups, 2)), sem((groups, 2)),
                sem((chips, groups, 2)), sem((chips, groups, 2)),
                sem((chips, groups, 2)), sem((chips, groups, 2)),
                sem((n_blk,)), sem((n_blk,)),
                sem((groups,)), sem((groups,)),
                sem((n_blk,)), sem((n_blk,)),
                sem((groups,)), sem((groups,)),
            ],
            compiler_params=pltpu.CompilerParams(
                collective_id=0, has_side_effects=True, vmem_limit_bytes=48 * 1024 * 1024
            ),
        )(
            embeddings,
            cluster_ids.reshape(1, rows),
            order_index.reshape(1, rows),
            shard_counts.reshape(1, 1),
        )
        return best.reshape(rows), centroid

    placed = (
        P(("dp", "blk", "cent"), None),
        P(("dp", "blk", "cent"), None),
        P(("dp", "blk", "cent")),
        P(("dp", "blk", "cent")),
    )
    return jax.shard_map(
        on_device,
        mesh=mesh,
        in_specs=placed,
        out_specs=(P(("dp", "blk", "cent")), P(("dp", "cent"), "blk")),
        check_vma=False,
    )
```
